32 devices in a mesh: dp: 4 (over y, x), fsdp: 8 (over z, core).
Axes of the slice: x: 2, y: 2, z: 4, core: 2. Of those that a mesh axis runs over, the one named last changes fastest.
Arguments:
- gradient: bfloat16 [4, 4096, 2, 1024], P('dp', 'fsdp'), may hold values from -3 to 3
- block_owner_index: int32 [8], replicated, may hold values from 0 to 7, as said below
- block_grid_cell: int32 [8], replicated, may hold values from 0 to 7, each once
- left_eigen_basis: float32 [16, 1024, 1024], P('fsdp', None, 'dp'), may hold values from -0.1875 to 0.1875
- right_eigen_basis: float32 [16, 1024, 1024], P('fsdp', None, 'dp'), may hold values from -0.1875 to 0.1875
- left_statistic_matrix: float32 [16, 1024, 1024], P('fsdp', None, 'dp'), may hold values from -6 to 6
- right_statistic_matrix: float32 [16, 1024, 1024], P('fsdp', None, 'dp'), may hold values from -6 to 6
- first_adam_moment: float32 [16, 1024, 1024], P('fsdp', None, 'dp'), may hold values from -0.09 to 0.09
- second_adam_moment: float32 [16, 1024, 1024], P('fsdp', None, 'dp'), may hold values from 1e-05 to 0.001
Outputs:
- new_left_stat: float32 [16, 1024, 1024], P('fsdp', None, 'dp')
- new_right_stat: float32 [16, 1024, 1024], P('fsdp', None, 'dp')
- new_first: float32 [16, 1024, 1024], P('fsdp', None, 'dp')
- new_second: float32 [16, 1024, 1024], P('fsdp', None, 'dp')
- update: bfloat16 [4096, 2, 1024], P('fsdp', None, 'dp')
The draws below stay inside these ranges and needn't reach their ends.
Inputs may be any that keep to these rules, and one draw needn't show every extreme that they name: `block_owner_index`: no fsdp index owns more than 2 blocks; a quarter of the fsdp indices own 2 blocks and a quarter own none.
All inputs are finite; a program needn't handle non-finite values.
Results may differ from the reference program's by a relative error of at most 0.013.
Values may be sent and summed in bfloat16 or wider, within the bound.
A program may use at most 128 MiB of HBM per device.

```python
import math
import jax
import jax.numpy as jnp
from jax import lax

BLOCK_ORDER = 1024
ROWS = 4096
SLOTS = 2
NBC = 2
NBLK = 8
SLOT_TOTAL = 16
N_DP = 4
N_FSDP = 8


def draw_block_owner_index(key, part):
    first_key, second_key = jax.random.split(jax.random.fold_in(key, 7))
    order = jax.random.permutation(first_key, N_FSDP)
    heavy = N_FSDP // 4
    places = jnp.arange(N_FSDP, dtype=jnp.int32)
    position = jnp.where(places < 2 * heavy, places // 2, places - heavy)
    listed = order[position]
    shuffle = jax.random.permutation(second_key, N_FSDP)
    return listed[shuffle].astype(jnp.int32)


def draw_gradient(key, part):
    keys = jax.random.split(jax.random.fold_in(key, 11), 4)
    sigma = 3.5 / math.sqrt(BLOCK_ORDER)
    factors = 4
    noise = jax.random.normal(keys[0], (N_DP, ROWS, NBC, BLOCK_ORDER), jnp.float32) * (sigma / math.sqrt(N_DP))
    picked = jax.random.permutation(keys[1], N_DP)
    quarter = jnp.arange(BLOCK_ORDER, dtype=jnp.int32) // (BLOCK_ORDER // N_DP)
    boost = jnp.where(quarter[None, :] == picked[:, None], 2.5, 1.0).astype(jnp.float32)
    noise = noise * boost[:, None, None, :]
    row_factor = jax.random.normal(keys[2], (ROWS, factors), jnp.float32)
    col_factor = jax.random.normal(keys[3], (factors, NBC, BLOCK_ORDER), jnp.float32)
    common = jnp.einsum('rk,knj->rnj', row_factor, col_factor) * (sigma / math.sqrt(factors))
    value = noise + common[None] / N_DP
    return jnp.clip(value, -3.0, 3.0).astype(jnp.bfloat16)


def steps_of(stream_key, dims, cuts, low, largest):
    factor_of = 1.0
    for dim, parts in cuts:
        heights = jax.random.uniform(jax.random.fold_in(jax.random.fold_in(stream_key, 6), dim), (parts,), jnp.float32, low / len(cuts), largest / len(cuts))
        factor_of = factor_of * jnp.repeat(jnp.exp(heights), dims[dim] // parts).reshape((-1,) + (1,) * (len(dims) - 1 - dim))
    return factor_of


def normal_values(rng, extent, scale, bound, shards=(), held_as=jnp.bfloat16):
    values = jax.random.normal(rng, extent, jnp.float32) * scale
    if len(shards) > 0:
        values = steps_of(rng, extent, shards, -0.22, 0.18) * values
    return jnp.clip(values, min=-bound, max=bound).astype(held_as)


def setup_inputs(seed: int = 0) -> dict:
    streams_of = jax.random.split(jax.random.key(seed), 10)
    return {
        "gradient": draw_gradient(jax.random.fold_in(streams_of[9], 71), 0),
        "block_owner_index": draw_block_owner_index(jax.random.fold_in(streams_of[9], 71), 0),
        "block_grid_cell": jax.random.permutation(streams_of[2], NBLK).astype(jnp.int32),
        "left_eigen_basis": normal_values(streams_of[3], (SLOT_TOTAL, BLOCK_ORDER, BLOCK_ORDER), BLOCK_ORDER ** -0.5, 0.1875, ((0, 8), (2, 4)), jnp.float32),
        "right_eigen_basis": normal_values(streams_of[4], (SLOT_TOTAL, BLOCK_ORDER, BLOCK_ORDER), BLOCK_ORDER ** -0.5, 0.1875, ((0, 8), (2, 4)), jnp.float32),
        "left_statistic_matrix": normal_values(streams_of[5], (SLOT_TOTAL, BLOCK_ORDER, BLOCK_ORDER), 1.0, 6.0, ((0, 8), (2, 4)), jnp.float32),
        "right_statistic_matrix": normal_values(streams_of[6], (SLOT_TOTAL, BLOCK_ORDER, BLOCK_ORDER), 1.0, 6.0, ((0, 8), (2, 4)), jnp.float32),
        "first_adam_moment": normal_values(streams_of[7], (SLOT_TOTAL, BLOCK_ORDER, BLOCK_ORDER), 0.015, 0.09, ((0, 8), (2, 4)), jnp.float32),
        "second_adam_moment": jnp.clip(jnp.exp(math.log(0.001) - 4.6051703 * jax.random.uniform(streams_of[8], (SLOT_TOTAL, BLOCK_ORDER, BLOCK_ORDER), jnp.float32) ** steps_of(streams_of[8], (SLOT_TOTAL, BLOCK_ORDER, BLOCK_ORDER), ((0, 8), (2, 4)), -0.2, 0.2)), 9.999999747378752e-06, 0.001),
    }


def slot_lookup_table(block_owner_index, block_grid_cell, slot_count):
    block_ids = jnp.arange(block_owner_index.shape[0], dtype=jnp.int32)
    shared = (block_owner_index[:, None] == block_owner_index[None, :]) & (block_ids[None, :] < block_ids[:, None])
    rank_in = lax.optimization_barrier(jnp.sum(shared.astype(jnp.int32), axis=1))
    block_slot_index = block_owner_index * SLOTS + rank_in
    slot_ids = jnp.arange(slot_count, dtype=jnp.int32)
    matches = (block_slot_index[None, :] == slot_ids[:, None]).astype(jnp.int32)
    filled_marker = lax.optimization_barrier(jnp.sum(matches, axis=1))
    slot_grid_cell = lax.optimization_barrier(jnp.sum(matches * block_grid_cell[None, :], axis=1))
    return (block_slot_index, filled_marker, slot_grid_cell)

def reference(gradient, block_owner_index, block_grid_cell, left_eigen_basis, right_eigen_basis, left_statistic_matrix, right_statistic_matrix, first_adam_moment, second_adam_moment):
    highest = lax.Precision.HIGHEST
    summed = lax.optimization_barrier(jnp.sum(gradient.astype(jnp.float32), axis=0)).astype(jnp.bfloat16)
    grid_rows = ROWS // BLOCK_ORDER
    blocks = summed.reshape(grid_rows, BLOCK_ORDER, NBC, BLOCK_ORDER)
    block_slot_index, filled_marker, slot_grid_cell = slot_lookup_table(block_owner_index, block_grid_cell, SLOT_TOTAL)
    anchor = jnp.zeros((), jnp.int32)

    def one_slot(items):
        filled_one, cell_one, left_one, right_one, lstat, rstat, first_one, second_one = items
        row_at = (cell_one // NBC).astype(jnp.int32)
        col_at = (cell_one % NBC).astype(jnp.int32)
        piece = lax.dynamic_slice(blocks, (row_at, anchor, col_at, anchor), (1, BLOCK_ORDER, 1, BLOCK_ORDER)).reshape(BLOCK_ORDER, BLOCK_ORDER)
        piece = jnp.where(filled_one > 0, piece, jnp.zeros_like(piece))
        new_left = 0.95 * lstat + 0.05 * jnp.dot(piece, piece.T, preferred_element_type=jnp.float32)
        new_right = 0.95 * rstat + 0.05 * jnp.dot(piece.T, piece, preferred_element_type=jnp.float32)
        half_turn = jnp.dot(left_one.T, piece.astype(jnp.float32), precision=highest).astype(jnp.bfloat16)
        turned = jnp.dot(half_turn.astype(jnp.float32), right_one, precision=highest)
        new_first = 0.9 * first_one + 0.1 * turned
        new_second = 0.999 * second_one + 0.001 * turned * turned
        direction = new_first / (jnp.sqrt(new_second) + 1e-08)
        mixed = jnp.dot(direction, right_one.T, precision=highest)
        back = jnp.dot(left_one, mixed, precision=highest).astype(jnp.bfloat16)
        return (new_left, new_right, new_first, new_second, back)
    new_left, new_right, new_first, new_second, backs = lax.map(one_slot, (filled_marker, slot_grid_cell, left_eigen_basis, right_eigen_basis, left_statistic_matrix, right_statistic_matrix, first_adam_moment, second_adam_moment))
    cells = jnp.arange(NBLK, dtype=jnp.int32)
    cell_hits = (block_grid_cell[None, :] == cells[:, None]).astype(jnp.int32)
    slot_for_cell = lax.optimization_barrier(jnp.sum(cell_hits * block_slot_index[None, :], axis=1))
    picked = jnp.take(backs, slot_for_cell, axis=0)
    update = picked.reshape(grid_rows, NBC, BLOCK_ORDER, BLOCK_ORDER).transpose(0, 2, 1, 3).reshape(ROWS, NBC, BLOCK_ORDER)
    return (new_left, new_right, new_first, new_second, update)
```

```python
import jax
import jax.numpy as jnp
from jax import lax
from jax.sharding import PartitionSpec as P


def slot_lookup_table(block_owner_index, block_grid_cell, slot_count, per_owner):
    block_ids = jnp.arange(block_owner_index.shape[0], dtype=jnp.int32)
    shared = (block_owner_index[:, None] == block_owner_index[None, :]) & (
        block_ids[None, :] < block_ids[:, None]
    )
    rank_in = jnp.sum(shared.astype(jnp.int32), axis=1)
    block_slot_index = block_owner_index * per_owner + rank_in
    slot_ids = jnp.arange(slot_count, dtype=jnp.int32)
    matches = (block_slot_index[None, :] == slot_ids[:, None]).astype(jnp.int32)
    filled_marker = jnp.sum(matches, axis=1)
    slot_grid_cell = jnp.sum(matches * block_grid_cell[None, :], axis=1)
    return (filled_marker, slot_grid_cell)


def local(
    gradient,
    block_owner_index,
    block_grid_cell,
    left_eigen_basis,
    right_eigen_basis,
    left_statistic_matrix,
    right_statistic_matrix,
    first_adam_moment,
    second_adam_moment,
):
    bf16, f32 = jnp.bfloat16, jnp.float32
    replicas = lax.axis_size("dp")
    members = lax.axis_size("fsdp")
    member = lax.axis_index("fsdp")
    column_group = lax.axis_index("dp")
    per_owner, block, width = left_eigen_basis.shape
    band_rows, grid_cols = gradient.shape[1:3]
    bands = block // band_rows
    grid_rows = members // bands
    cells = grid_rows * grid_cols

    filled_marker, slot_grid_cell = slot_lookup_table(
        block_owner_index, block_grid_cell, per_owner * members, per_owner
    )
    my_filled = lax.dynamic_slice_in_dim(filled_marker, member * per_owner, per_owner, 0)
    my_cell = lax.dynamic_slice_in_dim(slot_grid_cell, member * per_owner, per_owner, 0)

    left = left_eigen_basis.astype(bf16)
    right = right_eigen_basis.astype(bf16)
    left_full = lax.all_gather(left, "dp", axis=2, tiled=True)

    terms = jnp.transpose(
        gradient.reshape(band_rows, grid_cols, replicas, width), (2, 1, 0, 3)
    ).reshape(replicas * grid_cols * band_rows, width)
    reduced = lax.psum_scatter(terms, "dp", scatter_dimension=0, tiled=True)
    everyone = lax.all_gather(reduced, "fsdp", axis=0, tiled=True)
    everyone = everyone.reshape(grid_rows, bands, grid_cols, band_rows, width)
    pieces = []
    for k in range(per_owner):
        cell = my_cell[k]
        piece = lax.dynamic_slice(
            everyone,
            (cell // grid_cols, 0, cell % grid_cols, 0, 0),
            (1, bands, 1, band_rows, width),
        ).reshape(block, width)
        pieces.append(jnp.where(my_filled[k] > 0, piece, jnp.zeros_like(piece)))
    col_piece = jnp.stack(pieces)
    gathered = lax.all_gather(col_piece, "dp", axis=2, tiled=True)
    row_piece = lax.dynamic_slice_in_dim(gathered, column_group * width, width, 1)

    turned_right = jnp.einsum(
        "skj,sjc->skc", gathered, right, preferred_element_type=f32
    ).astype(bf16)
    turned = jnp.einsum("ski,skc->sic", left_full, turned_right, preferred_element_type=f32)
    new_first = 0.9 * first_adam_moment + 0.1 * turned
    new_second = 0.999 * second_adam_moment + 0.001 * turned * turned
    direction = (new_first / (jnp.sqrt(new_second) + 1e-08)).astype(bf16)
    mixed = jnp.einsum("sik,skc->sic", left_full, direction, preferred_element_type=f32).astype(bf16)
    partial = jnp.einsum(
        "sic,sdjc->dsij",
        mixed,
        right.reshape(per_owner, replicas, width, width),
        preferred_element_type=f32,
    ).astype(bf16)
    back = lax.psum_scatter(
        partial.reshape(replicas * per_owner * block, width), "dp", scatter_dimension=0, tiled=True
    ).reshape(per_owner, bands, band_rows, width)

    new_left = 0.95 * left_statistic_matrix + 0.05 * jnp.einsum(
        "sik,sjk->sij", gathered, row_piece, preferred_element_type=f32
    )
    new_right = 0.95 * right_statistic_matrix + 0.05 * jnp.einsum(
        "ski,skj->sij", gathered, col_piece, preferred_element_type=f32
    )

    placed = []
    for cell in range(cells):
        here = jnp.zeros((bands, band_rows, width), bf16)
        for k in range(per_owner):
            here = jnp.where((my_filled[k] > 0) & (my_cell[k] == cell), back[k], here)
        placed.append(here)
    placed = jnp.stack(placed).reshape(grid_rows, grid_cols, bands, band_rows, width)
    placed = jnp.transpose(placed, (0, 2, 1, 3, 4)).reshape(members * grid_cols * band_rows, width)
    mine = lax.psum_scatter(placed, "fsdp", scatter_dimension=0, tiled=True)
    update = jnp.transpose(mine.reshape(grid_cols, band_rows, width), (1, 0, 2))
    return (new_left, new_right, new_first, new_second, update)


def solution(mesh):
    slots = P("fsdp", None, "dp")
    in_specs = (P("dp", "fsdp", None, None), P(), P()) + (slots,) * 6
    return jax.shard_map(
        local, mesh=mesh, in_specs=in_specs, out_specs=(slots,) * 5, check_vma=False
    )
```

```python
import functools

import jax
import jax.numpy as jnp
from jax import lax
from jax.experimental import pallas as pl
from jax.experimental.pallas import tpu as pltpu
from jax.sharding import PartitionSpec as P

MESH = pl.DeviceIdType.MESH


def meet(replicas, members, d, m):
    barrier = pltpu.get_barrier_semaphore()
    for o in range(1, replicas):
        pl.semaphore_signal(
            barrier, inc=1, device_id={"dp": lax.rem(d + o, replicas)}, device_id_type=MESH
        )
    for o in range(1, members):
        pl.semaphore_signal(
            barrier, inc=1, device_id={"fsdp": lax.rem(m + o, members)}, device_id_type=MESH
        )
    pl.semaphore_wait(barrier, replicas + members - 2)


def push(src, dst, send, recv, axis, to):
    copy = pltpu.make_async_remote_copy(
        src_ref=src,
        dst_ref=dst,
        send_sem=send,
        recv_sem=recv,
        device_id={axis: to},
        device_id_type=MESH,
    )
    copy.start()
    return copy


def spread_first(full, mine, d, sems):
    width = mine.shape[2]
    here = full.at[:, :, pl.ds(pl.multiple_of(d * width, width), width)]
    own = pltpu.make_async_copy(mine, here, sems.at[2, 0])
    own.start()
    one = push(mine, here, sems.at[0, 0], sems.at[1, 0], "dp", d + 1 - 2 * lax.rem(d, 2))
    two = push(mine, here, sems.at[0, 1], sems.at[1, 1], "dp", lax.rem(d + 2, 4))
    return own, one, two


def spread_relay(full, width, d, sems, first):
    half = full.shape[1] // 2
    d1 = d + 1 - 2 * lax.rem(d, 2)
    d2 = lax.rem(d + 2, 4)
    first[1].wait_recv()
    top = full.at[:, pl.ds(0, half), pl.ds(pl.multiple_of(d1 * width, width), width)]
    a = push(top, top, sems.at[0, 2], sems.at[1, 2], "dp", d2)
    first[2].wait_recv()
    low = full.at[:, pl.ds(half, half), pl.ds(pl.multiple_of(d2 * width, width), width)]
    b = push(low, low, sems.at[0, 3], sems.at[1, 3], "dp", d1)
    return a, b


def bring_kernel(
    replicas, members, at_ref, fill_ref, terms, left, gath, leftf, col,
    inbox, red, p1, p2, rs, s1, s2, gs, ls,
):
    d, m = lax.axis_index("dp"), lax.axis_index("fsdp")
    per_owner, block, width = left.shape
    grid_cols, piece = terms.shape[2:4]
    bands = p2.shape[2]
    f32, bf16 = jnp.float32, jnp.bfloat16
    meet(replicas, members, d, m)
    sums = []
    for o in range(1, replicas):
        to = lax.rem(d + o, replicas)
        sums.append(push(terms.at[to], inbox.at[d], rs.at[0, o], rs.at[1, o], "dp", to))
    for c in sums:
        c.wait_recv()
    out = []
    for p in range(members):
        to = lax.rem(m + p, members)
        acc = terms[d, to].astype(f32)
        for o in range(1, replicas):
            acc += inbox[lax.rem(d + o, replicas), to].astype(f32)
        if p:
            red[to] = acc.astype(bf16)
            out.append(
                push(
                    red.at[to], p1.at[pl.ds(m * grid_cols, grid_cols)],
                    s1.at[0, p], s1.at[1, p], "fsdp", to,
                )
            )
        else:
            p1[pl.ds(m * grid_cols, grid_cols)] = acc.astype(bf16)
    lfirst = spread_first(leftf, left, d, ls)
    for c in out:
        c.wait_recv()
    out2 = []
    for p in range(members):
        to = lax.rem(m + p, members)
        for k in range(per_owner):
            keep = fill_ref[to * per_owner + k]
            for b in range(bands):
                got = p1[at_ref[(to * per_owner + k) * bands + b]]
                got = (got.astype(f32) * keep).astype(bf16)
                if p:
                    p2[to, k, b] = got
                else:
                    col[k, b, m] = got
        if p:
            out2.append(
                push(p2.at[to], col.at[:, :, m], s2.at[0, p], s2.at[1, p], "fsdp", to)
            )
    lrelay = spread_relay(leftf, width, d, ls, lfirst)
    for c in out2:
        c.wait_recv()
    mine = col.reshape(per_owner, block, width)
    gfirst = spread_first(gath, mine, d, gs)
    grelay = spread_relay(gath, width, d, gs, gfirst)
    for c in lrelay + grelay:
        c.wait_recv()
    for c in sums + out + out2 + list(lfirst[1:] + lrelay + gfirst[1:] + grelay):
        c.wait_send()
    lfirst[0].wait()
    gfirst[0].wait()


def bring(terms, left, at, fill):
    replicas, members, grid_cols, piece, width = terms.shape
    per_owner, block, _ = left.shape
    bands = block // (members * piece)
    bf16, dma = jnp.bfloat16, pltpu.SemaphoreType.DMA
    vmem = pl.BlockSpec(memory_space=pltpu.VMEM)
    smem = pl.BlockSpec(memory_space=pltpu.SMEM)
    full = jax.ShapeDtypeStruct((per_owner, block, replicas * width), bf16)
    return pl.pallas_call(
        functools.partial(bring_kernel, replicas, members),
        out_shape=(
            full, full,
            jax.ShapeDtypeStruct((per_owner, bands, members, piece, width), bf16),
        ),
        in_specs=[smem, smem, vmem, vmem],
        out_specs=(vmem, vmem, vmem),
        scratch_shapes=[
            pltpu.VMEM(terms.shape, bf16),
            pltpu.VMEM(terms.shape[1:], bf16),
            pltpu.VMEM((members * grid_cols, piece, width), bf16),
            pltpu.VMEM((members, per_owner, bands, piece, width), bf16),
            dma((2, replicas)), dma((2, members)), dma((2, members)), dma((3, 4)), dma((3, 4)),
        ],
        compiler_params=pltpu.CompilerParams(
            collective_id=0, has_side_effects=True, vmem_limit_bytes=40 * 2**20
        ),
    )(at, fill, terms, left)


def home_kernel(replicas, members, at_ref, partial, upd, inbox, bk, h1, p2, rs, s1, s2):
    d, m = lax.axis_index("dp"), lax.axis_index("fsdp")
    per_owner, bands = partial.shape[1:3]
    grid_cols = upd.shape[1]
    f32, bf16 = jnp.float32, jnp.bfloat16
    meet(replicas, members, d, m)
    sums, out, out2 = [], [], []
    for k in range(per_owner):
        for o in range(1, replicas):
            to = lax.rem(d + o, replicas)
            sums.append(
                push(partial.at[to, k], inbox.at[d, k], rs.at[0, k, o], rs.at[1, k, o], "dp", to)
            )
    for k in range(per_owner):
        for o in range(1, replicas):
            sums[k * (replicas - 1) + o - 1].wait_recv()
        for p in range(members):
            to = lax.rem(m + p, members)
            acc = partial[d, k, :, to].astype(f32)
            for o in range(1, replicas):
                acc += inbox[lax.rem(d + o, replicas), k, :, to].astype(f32)
            if p:
                bk[k, to] = acc.astype(bf16)
                out.append(
                    push(
                        bk.at[k, to],
                        h1.at[pl.ds((m * per_owner + k) * bands, bands)],
                        s1.at[0, k, p], s1.at[1, k, p], "fsdp", to,
                    )
                )
            else:
                h1[pl.ds((m * per_owner + k) * bands, bands)] = acc.astype(bf16)
    for c in out:
        c.wait_recv()
    for p in range(members):
        to = lax.rem(m + p, members)
        for c in range(grid_cols):
            got = h1[at_ref[to * grid_cols + c]]
            if p:
                p2[to, c] = got
            else:
                upd[m, c] = got
        if p:
            out2.append(push(p2.at[to], upd.at[m], s2.at[0, p], s2.at[1, p], "fsdp", to))
    for c in out2:
        c.wait_recv()
    for c in sums + out + out2:
        c.wait_send()


def home(partial, at, grid_cols):
    replicas, per_owner, bands, members, piece, width = partial.shape
    bf16, dma = jnp.bfloat16, pltpu.SemaphoreType.DMA
    vmem = pl.BlockSpec(memory_space=pltpu.VMEM)
    return pl.pallas_call(
        functools.partial(home_kernel, replicas, members),
        out_shape=jax.ShapeDtypeStruct((members, grid_cols, piece, width), bf16),
        in_specs=[pl.BlockSpec(memory_space=pltpu.SMEM), vmem],
        out_specs=vmem,
        scratch_shapes=[
            pltpu.VMEM(partial.shape, bf16),
            pltpu.VMEM((per_owner, members, bands, piece, width), bf16),
            pltpu.VMEM((members * per_owner * bands, piece, width), bf16),
            pltpu.VMEM((members, grid_cols, piece, width), bf16),
            dma((2, per_owner, replicas)), dma((2, per_owner, members)), dma((2, members)),
        ],
        compiler_params=pltpu.CompilerParams(
            collective_id=1, has_side_effects=True, vmem_limit_bytes=40 * 2**20
        ),
    )(at, partial)


def slot_lookup_table(block_owner_index, block_grid_cell, slot_count, per_owner):
    block_ids = jnp.arange(block_owner_index.shape[0], dtype=jnp.int32)
    shared = (block_owner_index[:, None] == block_owner_index[None, :]) & (
        block_ids[None, :] < block_ids[:, None]
    )
    rank_in = jnp.sum(shared.astype(jnp.int32), axis=1)
    block_slot_index = block_owner_index * per_owner + rank_in
    slot_ids = jnp.arange(slot_count, dtype=jnp.int32)
    matches = (block_slot_index[None, :] == slot_ids[:, None]).astype(jnp.int32)
    filled_marker = jnp.sum(matches, axis=1)
    slot_grid_cell = jnp.sum(matches * block_grid_cell[None, :], axis=1)
    return (block_slot_index, filled_marker, slot_grid_cell)


def local(
    gradient,
    block_owner_index,
    block_grid_cell,
    left_eigen_basis,
    right_eigen_basis,
    left_statistic_matrix,
    right_statistic_matrix,
    first_adam_moment,
    second_adam_moment,
):
    bf16, f32 = jnp.bfloat16, jnp.float32
    replicas = lax.axis_size("dp")
    members = lax.axis_size("fsdp")
    member = lax.axis_index("fsdp")
    column_group = lax.axis_index("dp")
    per_owner, block, width = left_eigen_basis.shape
    band_rows, grid_cols = gradient.shape[1:3]
    bands = block // band_rows
    grid_rows = members // bands
    cells = grid_rows * grid_cols

    block_slot_index, filled_marker, slot_grid_cell = slot_lookup_table(
        block_owner_index, block_grid_cell, per_owner * members, per_owner
    )
    my_filled = lax.dynamic_slice_in_dim(filled_marker, member * per_owner, per_owner, 0)
    my_cell = lax.dynamic_slice_in_dim(slot_grid_cell, member * per_owner, per_owner, 0)

    left = left_eigen_basis.astype(bf16)
    right = right_eigen_basis.astype(bf16)
    piece_rows = band_rows // members
    direct = replicas == 4 and band_rows % members == 0 and piece_rows % 16 == 0
    if direct:
        terms = jnp.transpose(
            gradient.reshape(members, piece_rows, grid_cols, replicas, width), (3, 0, 2, 1, 4)
        )
        part = jnp.arange(bands, dtype=jnp.int32)[None, :]
        at = (
            (slot_grid_cell // grid_cols * bands)[:, None] + part
        ) * grid_cols + (slot_grid_cell % grid_cols)[:, None]
        gathered, left_full, col_piece = bring(
            terms, left, at.reshape(-1), (filled_marker > 0).astype(f32)
        )
        col_piece = col_piece.reshape(per_owner, block, width)
    else:
        left_full = lax.all_gather(left, "dp", axis=2, tiled=True)

        terms = jnp.transpose(
            gradient.reshape(band_rows, grid_cols, replicas, width), (2, 1, 0, 3)
        ).reshape(replicas * grid_cols * band_rows, width)
        reduced = lax.psum_scatter(terms, "dp", scatter_dimension=0, tiled=True)
        everyone = lax.all_gather(reduced, "fsdp", axis=0, tiled=True)
        everyone = everyone.reshape(grid_rows, bands, grid_cols, band_rows, width)
        pieces = []
        for k in range(per_owner):
            cell = my_cell[k]
            piece = lax.dynamic_slice(
                everyone,
                (cell // grid_cols, 0, cell % grid_cols, 0, 0),
                (1, bands, 1, band_rows, width),
            ).reshape(block, width)
            pieces.append(jnp.where(my_filled[k] > 0, piece, jnp.zeros_like(piece)))
        col_piece = jnp.stack(pieces)
        gathered = lax.all_gather(col_piece, "dp", axis=2, tiled=True)
    row_piece = lax.dynamic_slice_in_dim(gathered, column_group * width, width, 1)

    turned_right = jnp.einsum(
        "skj,sjc->skc", gathered, right, preferred_element_type=f32
    ).astype(bf16)
    turned = jnp.einsum("ski,skc->sic", left_full, turned_right, preferred_element_type=f32)
    new_first = 0.9 * first_adam_moment + 0.1 * turned
    new_second = 0.999 * second_adam_moment + 0.001 * turned * turned
    direction = (new_first / (jnp.sqrt(new_second) + 1e-08)).astype(bf16)
    mixed = jnp.einsum("sik,skc->sic", left_full, direction, preferred_element_type=f32).astype(bf16)
    partial = jnp.einsum(
        "sic,sdjc->dsij",
        mixed,
        right.reshape(per_owner, replicas, width, width),
        preferred_element_type=f32,
    ).astype(bf16)
    new_left = 0.95 * left_statistic_matrix + 0.05 * jnp.einsum(
        "sik,sjk->sij", gathered, row_piece, preferred_element_type=f32
    )
    new_right = 0.95 * right_statistic_matrix + 0.05 * jnp.einsum(
        "ski,skj->sij", gathered, col_piece, preferred_element_type=f32
    )

    if direct:
        all_cells = jnp.arange(cells, dtype=jnp.int32)
        hits = (block_grid_cell[None, :] == all_cells[:, None]).astype(jnp.int32)
        cell_slot = jnp.sum(hits * block_slot_index[None, :], axis=1)
        at = cell_slot.reshape(grid_rows, 1, grid_cols) * bands + jnp.arange(
            bands, dtype=jnp.int32
        ).reshape(1, bands, 1)
        mine = home(
            partial.reshape(replicas, per_owner, bands, members, piece_rows, width),
            at.reshape(-1),
            grid_cols,
        )
        update = jnp.transpose(mine, (0, 2, 1, 3)).reshape(band_rows, grid_cols, width)
    else:
        back = lax.psum_scatter(
            partial.reshape(replicas * per_owner * block, width), "dp", scatter_dimension=0, tiled=True
        ).reshape(per_owner, bands, band_rows, width)

        placed = []
        for cell in range(cells):
            here = jnp.zeros((bands, band_rows, width), bf16)
            for k in range(per_owner):
                here = jnp.where((my_filled[k] > 0) & (my_cell[k] == cell), back[k], here)
            placed.append(here)
        placed = jnp.stack(placed).reshape(grid_rows, grid_cols, bands, band_rows, width)
        placed = jnp.transpose(placed, (0, 2, 1, 3, 4)).reshape(members * grid_cols * band_rows, width)
        mine = lax.psum_scatter(placed, "fsdp", scatter_dimension=0, tiled=True)
        update = jnp.transpose(mine.reshape(grid_cols, band_rows, width), (1, 0, 2))
    return (new_left, new_right, new_first, new_second, update)


def solution(mesh):
    slots = P("fsdp", None, "dp")
    in_specs = (P("dp", "fsdp", None, None), P(), P()) + (slots,) * 6
    return jax.shard_map(
        local, mesh=mesh, in_specs=in_specs, out_specs=(slots,) * 5, check_vma=False
    )
```

```python
import functools

import jax
import jax.numpy as jnp
from jax import lax
from jax.experimental import pallas as pl
from jax.experimental.pallas import tpu as pltpu
from jax.sharding import PartitionSpec as P

MESH = pl.DeviceIdType.MESH


def meet(replicas, members, d, m):
    barrier = pltpu.get_barrier_semaphore()
    for o in range(1, replicas):
        pl.semaphore_signal(
            barrier, inc=1, device_id={"dp": lax.rem(d + o, replicas)}, device_id_type=MESH
        )
    for o in range(1, members):
        pl.semaphore_signal(
            barrier, inc=1, device_id={"fsdp": lax.rem(m + o, members)}, device_id_type=MESH
        )
    pl.semaphore_wait(barrier, replicas + members - 2)


def push(src, dst, send, recv, axis, to):
    copy = pltpu.make_async_remote_copy(
        src_ref=src,
        dst_ref=dst,
        send_sem=send,
        recv_sem=recv,
        device_id={axis: to},
        device_id_type=MESH,
    )
    copy.start()
    return copy


def spread_first(full, mine, d, sems):
    width = mine.shape[2]
    here = full.at[:, :, pl.ds(pl.multiple_of(d * width, width), width)]
    own = pltpu.make_async_copy(mine, here, sems.at[2, 0])
    own.start()
    one = push(mine, here, sems.at[0, 0], sems.at[1, 0], "dp", d + 1 - 2 * lax.rem(d, 2))
    two = push(mine, here, sems.at[0, 1], sems.at[1, 1], "dp", lax.rem(d + 2, 4))
    return own, one, two


def spread_relay(full, width, d, sems, first):
    half = full.shape[1] // 2
    d1 = d + 1 - 2 * lax.rem(d, 2)
    d2 = lax.rem(d + 2, 4)
    first[1].wait_recv()
    top = full.at[:, pl.ds(0, half), pl.ds(pl.multiple_of(d1 * width, width), width)]
    a = push(top, top, sems.at[0, 2], sems.at[1, 2], "dp", d2)
    first[2].wait_recv()
    low = full.at[:, pl.ds(half, half), pl.ds(pl.multiple_of(d2 * width, width), width)]
    b = push(low, low, sems.at[0, 3], sems.at[1, 3], "dp", d1)
    return a, b


def bring_kernel(
    replicas, members, at_ref, fill_ref, terms, left, gath, leftf,
    col, inbox, red, p1, p2, rs, s1, s2, gs, ls,
):
    d, m = lax.axis_index("dp"), lax.axis_index("fsdp")
    per_owner, block, width = left.shape
    grid_cols, piece = terms.shape[2:4]
    bands = p2.shape[2]
    f32, bf16 = jnp.float32, jnp.bfloat16
    meet(replicas, members, d, m)
    sums = []
    for o in range(1, replicas):
        to = lax.rem(d + o, replicas)
        sums.append(push(terms.at[to], inbox.at[d], rs.at[0, o], rs.at[1, o], "dp", to))
    for c in sums:
        c.wait_recv()
    out = []
    for p in range(members):
        to = lax.rem(m + p, members)
        acc = terms[d, to].astype(f32)
        for o in range(1, replicas):
            acc += inbox[lax.rem(d + o, replicas), to].astype(f32)
        if p:
            red[to] = acc.astype(bf16)
            out.append(
                push(
                    red.at[to], p1.at[pl.ds(m * grid_cols, grid_cols)],
                    s1.at[0, p], s1.at[1, p], "fsdp", to,
                )
            )
        else:
            p1[pl.ds(m * grid_cols, grid_cols)] = acc.astype(bf16)
    lfirst = spread_first(leftf, left, d, ls)
    for c in out:
        c.wait_recv()
    out2 = []
    for p in range(members):
        to = lax.rem(m + p, members)
        for k in range(per_owner):
            keep = fill_ref[to * per_owner + k]
            for b in range(bands):
                got = p1[at_ref[(to * per_owner + k) * bands + b]]
                got = (got.astype(f32) * keep).astype(bf16)
                if p:
                    p2[to, k, b] = got
                else:
                    col[k, b, m] = got
        if p:
            out2.append(
                push(p2.at[to], col.at[:, :, m], s2.at[0, p], s2.at[1, p], "fsdp", to)
            )
    lrelay = spread_relay(leftf, width, d, ls, lfirst)
    for c in out2:
        c.wait_recv()
    mine = col.reshape(per_owner, block, width)
    gfirst = spread_first(gath, mine, d, gs)
    grelay = spread_relay(gath, width, d, gs, gfirst)
    for c in lrelay + grelay:
        c.wait_recv()
    for c in sums + out + out2 + list(lfirst[1:] + lrelay + gfirst[1:] + grelay):
        c.wait_send()
    lfirst[0].wait()
    gfirst[0].wait()


def bring(terms, left, at, fill):
    replicas, members, grid_cols, piece, width = terms.shape
    per_owner, block, _ = left.shape
    bands = block // (members * piece)
    bf16, dma = jnp.bfloat16, pltpu.SemaphoreType.DMA
    vmem = pl.BlockSpec(memory_space=pltpu.VMEM)
    smem = pl.BlockSpec(memory_space=pltpu.SMEM)
    full = jax.ShapeDtypeStruct((per_owner, block, replicas * width), bf16)
    return pl.pallas_call(
        functools.partial(bring_kernel, replicas, members),
        out_shape=(full, full),
        in_specs=[smem, smem, vmem, vmem],
        out_specs=(vmem, vmem),
        scratch_shapes=[
            pltpu.VMEM((per_owner, bands, members, piece, width), bf16),
            pltpu.VMEM(terms.shape, bf16),
            pltpu.VMEM(terms.shape[1:], bf16),
            pltpu.VMEM((members * grid_cols, piece, width), bf16),
            pltpu.VMEM((members, per_owner, bands, piece, width), bf16),
            dma((2, replicas)), dma((2, members)), dma((2, members)), dma((3, 4)), dma((3, 4)),
        ],
        compiler_params=pltpu.CompilerParams(
            collective_id=0, has_side_effects=True, vmem_limit_bytes=40 * 2**20
        ),
    )(at, fill, terms, left)


def home_kernel(
    replicas, members, at_ref, gath, leftf, right, lstat, rstat, first, second,
    new_left, new_right, new_first, new_second, upd,
    rf, rb, tr, dr, partial, ina, inb, rel, ina2, inb2, bk, h1, p2, ld, rs, s1, s2,
):
    d, m = lax.axis_index("dp"), lax.axis_index("fsdp")
    per_owner, block, width = right.shape
    grid_cols, piece = upd.shape[1:3]
    bands = block // (members * piece)
    hb, half = bands // 2, block // 2
    f32, bf16 = jnp.float32, jnp.bfloat16
    d1 = d + 1 - 2 * lax.rem(d, 2)
    d2 = lax.rem(d + 2, 4)
    d3 = 3 - d
    loads = [
        pltpu.make_async_copy(s, t, ld.at[i])
        for i, (s, t) in enumerate(
            (
                (right, rf), (first, new_first), (second, new_second),
                (lstat, new_left), (rstat, new_right),
            )
        )
    ]
    for c in loads:
        c.start()
    meet(replicas, members, d, m)
    tiles = block // width
    mine = pl.ds(pl.multiple_of(d * width, width), width)

    def mul(x, y, dims):
        return lax.dot_general(x, y, (dims, ((), ())), preferred_element_type=f32)

    def tile(i):
        return pl.ds(pl.multiple_of(i * width, width), width)

    def turn(k):
        @pl.loop(0, tiles)
        def _(i):
            tr[tile(i)] = mul(gath[k, tile(i)], rb[k], ((1,), (0,))).astype(bf16)

        @pl.loop(0, tiles)
        def _(i):
            t = mul(leftf[k, :, tile(i)], tr[...], ((0,), (0,)))
            nf = 0.9 * new_first[k, tile(i)] + 0.1 * t
            ns = 0.999 * new_second[k, tile(i)] + 0.001 * t * t
            new_first[k, tile(i)] = nf
            new_second[k, tile(i)] = ns
            dr[tile(i)] = (nf / (jnp.sqrt(ns) + 1e-08)).astype(bf16)

        @pl.loop(0, tiles)
        def _(i):
            x = mul(leftf[k, tile(i)], dr[...], ((1,), (0,))).astype(bf16)
            for t in range(replicas):
                partial[t, k, tile(i)] = mul(
                    x, rb[k, t * width : (t + 1) * width], ((1,), (1,))
                ).astype(bf16)

    def stats(k):
        @pl.loop(0, tiles)
        def _(i):
            a = mul(gath[k, tile(i)], gath[k, mine], ((1,), (1,)))
            new_left[k, tile(i)] = 0.95 * new_left[k, tile(i)] + 0.05 * a
            c = mul(gath[k, :, tile(i)], gath[k, :, mine], ((0,), (0,)))
            new_right[k, tile(i)] = 0.95 * new_right[k, tile(i)] + 0.05 * c

    top, low = pl.ds(0, half), pl.ds(half, half)

    def launch(k):
        return [
            push(partial.at[d3, k, top], ina.at[k, 1], rs.at[0, k, 0], rs.at[1, k, 0], "dp", d1),
            push(partial.at[d3, k, low], inb.at[k, 1], rs.at[0, k, 1], rs.at[1, k, 1], "dp", d2),
            push(partial.at[d1, k, top], ina.at[k, 0], rs.at[0, k, 2], rs.at[1, k, 2], "dp", d1),
            push(partial.at[d2, k, low], inb.at[k, 0], rs.at[0, k, 3], rs.at[1, k, 3], "dp", d2),
        ]

    def relay(k, c):
        c[0].wait_recv()
        rel[k, 0] = (partial[d2, k, top].astype(f32) + ina[k, 1].astype(f32)).astype(bf16)
        a = push(rel.at[k, 0], ina2.at[k], rs.at[0, k, 4], rs.at[1, k, 4], "dp", d2)
        c[1].wait_recv()
        rel[k, 1] = (partial[d1, k, low].astype(f32) + inb[k, 1].astype(f32)).astype(bf16)
        b = push(rel.at[k, 1], inb2.at[k], rs.at[0, k, 5], rs.at[1, k, 5], "dp", d1)
        return [a, b]

    out, out2 = [], []

    def finish(k, c, r):
        for h in range(2):
            c[2 + h].wait_recv()
            r[h].wait_recv()
            near, far = ((ina, ina2), (inb, inb2))[h]
            for p in range(members):
                to = lax.rem(m + p, members)
                at = (m * per_owner + k) * bands + h * hb
                for q in range(hb):
                    row = pl.ds(pl.multiple_of((q * members + to) * piece, piece), piece)
                    own = pl.ds(pl.multiple_of(h * half + (q * members + to) * piece, piece), piece)
                    acc = (
                        partial[d, k, own].astype(f32)
                        + near[k, 0, row].astype(f32)
                        + far[k, row].astype(f32)
                    ).astype(bf16)
                    if p:
                        bk[k, h, to, q] = acc
                    else:
                        h1[at + q] = acc
                if p:
                    out.append(
                        push(
                            bk.at[k, h, to], h1.at[pl.ds(at, hb)],
                            s1.at[0, k, h, p], s1.at[1, k, h, p], "fsdp", to,
                        )
                    )

    loads[0].wait()
    rb[...] = rf[...].astype(bf16)
    loads[1].wait()
    loads[2].wait()
    sent, passed = [], []
    for k in range(per_owner):
        turn(k)
        sent.append(launch(k))
    loads[3].wait()
    loads[4].wait()
    for k in range(per_owner):
        stats(k)
        passed.append(relay(k, sent[k]))
    for k in range(per_owner):
        finish(k, sent[k], passed[k])
    for c in out:
        c.wait_recv()
    for p in range(members):
        to = lax.rem(m + p, members)
        for c in range(grid_cols):
            got = h1[at_ref[to * grid_cols + c]]
            if p:
                p2[to, c] = got
            else:
                upd[m, c] = got
        if p:
            out2.append(push(p2.at[to], upd.at[m], s2.at[0, p], s2.at[1, p], "fsdp", to))
    for c in out2:
        c.wait_recv()
    for c in sum(sent + passed, []) + out + out2:
        c.wait_send()


def home(at, gath, leftf, right, lstat, rstat, first, second, replicas, members, grid_cols, piece):
    per_owner, block, width = right.shape
    bands = block // (members * piece)
    bf16, f32, dma = jnp.bfloat16, jnp.float32, pltpu.SemaphoreType.DMA
    vmem = pl.BlockSpec(memory_space=pltpu.VMEM)
    whole = pl.BlockSpec(memory_space=pl.ANY)
    state = jax.ShapeDtypeStruct(right.shape, f32)
    half = (per_owner, 2, block // 2, width)
    return pl.pallas_call(
        functools.partial(home_kernel, replicas, members),
        out_shape=(state,) * 4
        + (jax.ShapeDtypeStruct((members, grid_cols, piece, width), bf16),),
        in_specs=[pl.BlockSpec(memory_space=pltpu.SMEM), vmem, vmem] + [whole] * 5,
        out_specs=(vmem,) * 5,
        scratch_shapes=[
            pltpu.VMEM(right.shape, f32),
            pltpu.VMEM(right.shape, bf16),
            pltpu.VMEM((block, width), bf16),
            pltpu.VMEM((block, width), bf16),
            pltpu.VMEM((replicas, per_owner, block, width), bf16),
            pltpu.VMEM(half, bf16),
            pltpu.VMEM(half, bf16),
            pltpu.VMEM(half, bf16),
            pltpu.VMEM((per_owner, block // 2, width), bf16),
            pltpu.VMEM((per_owner, block // 2, width), bf16),
            pltpu.VMEM((per_owner, 2, members, bands // 2, piece, width), bf16),
            pltpu.VMEM((members * per_owner * bands, piece, width), bf16),
            pltpu.VMEM((members, grid_cols, piece, width), bf16),
            dma((5,)), dma((2, per_owner, 6)), dma((2, per_owner, 2, members)), dma((2, members)),
        ],
        compiler_params=pltpu.CompilerParams(
            collective_id=1, has_side_effects=True, vmem_limit_bytes=48 * 2**20
        ),
    )(at, gath, leftf, right, lstat, rstat, first, second)


def slot_lookup_table(block_owner_index, block_grid_cell, slot_count, per_owner):
    block_ids = jnp.arange(block_owner_index.shape[0], dtype=jnp.int32)
    shared = (block_owner_index[:, None] == block_owner_index[None, :]) & (
        block_ids[None, :] < block_ids[:, None]
    )
    rank_in = jnp.sum(shared.astype(jnp.int32), axis=1)
    block_slot_index = block_owner_index * per_owner + rank_in
    slot_ids = jnp.arange(slot_count, dtype=jnp.int32)
    matches = (block_slot_index[None, :] == slot_ids[:, None]).astype(jnp.int32)
    filled_marker = jnp.sum(matches, axis=1)
    slot_grid_cell = jnp.sum(matches * block_grid_cell[None, :], axis=1)
    return (block_slot_index, filled_marker, slot_grid_cell)


def local(
    gradient,
    block_owner_index,
    block_grid_cell,
    left_eigen_basis,
    right_eigen_basis,
    left_statistic_matrix,
    right_statistic_matrix,
    first_adam_moment,
    second_adam_moment,
):
    bf16, f32 = jnp.bfloat16, jnp.float32
    replicas = lax.axis_size("dp")
    members = lax.axis_size("fsdp")
    member = lax.axis_index("fsdp")
    column_group = lax.axis_index("dp")
    per_owner, block, width = left_eigen_basis.shape
    band_rows, grid_cols = gradient.shape[1:3]
    bands = block // band_rows
    grid_rows = members // bands
    cells = grid_rows * grid_cols

    block_slot_index, filled_marker, slot_grid_cell = slot_lookup_table(
        block_owner_index, block_grid_cell, per_owner * members, per_owner
    )
    my_filled = lax.dynamic_slice_in_dim(filled_marker, member * per_owner, per_owner, 0)
    my_cell = lax.dynamic_slice_in_dim(slot_grid_cell, member * per_owner, per_owner, 0)

    left = left_eigen_basis.astype(bf16)
    right = right_eigen_basis.astype(bf16)
    piece_rows = band_rows // members
    direct = (
        replicas == 4 and bands % 2 == 0 and band_rows % members == 0 and piece_rows % 16 == 0
    )
    if direct:
        terms = jnp.transpose(
            gradient.reshape(members, piece_rows, grid_cols, replicas, width), (3, 0, 2, 1, 4)
        )
        part = jnp.arange(bands, dtype=jnp.int32)[None, :]
        at = (
            (slot_grid_cell // grid_cols * bands)[:, None] + part
        ) * grid_cols + (slot_grid_cell % grid_cols)[:, None]
        gathered, left_full = bring(
            terms, left, at.reshape(-1), (filled_marker > 0).astype(f32)
        )
        all_cells = jnp.arange(cells, dtype=jnp.int32)
        hits = (block_grid_cell[None, :] == all_cells[:, None]).astype(jnp.int32)
        cell_slot = jnp.sum(hits * block_slot_index[None, :], axis=1)
        at = cell_slot.reshape(grid_rows, 1, grid_cols) * bands + jnp.arange(
            bands, dtype=jnp.int32
        ).reshape(1, bands, 1)
        *states, mine = home(
            at.reshape(-1),
            gathered,
            left_full,
            right_eigen_basis,
            left_statistic_matrix,
            right_statistic_matrix,
            first_adam_moment,
            second_adam_moment,
            replicas,
            members,
            grid_cols,
            piece_rows,
        )
        update = jnp.transpose(mine, (0, 2, 1, 3)).reshape(band_rows, grid_cols, width)
        return (*states, update)
    left_full = lax.all_gather(left, "dp", axis=2, tiled=True)

    terms = jnp.transpose(
        gradient.reshape(band_rows, grid_cols, replicas, width), (2, 1, 0, 3)
    ).reshape(replicas * grid_cols * band_rows, width)
    reduced = lax.psum_scatter(terms, "dp", scatter_dimension=0, tiled=True)
    everyone = lax.all_gather(reduced, "fsdp", axis=0, tiled=True)
    everyone = everyone.reshape(grid_rows, bands, grid_cols, band_rows, width)
    pieces = []
    for k in range(per_owner):
        cell = my_cell[k]
        piece = lax.dynamic_slice(
            everyone,
            (cell // grid_cols, 0, cell % grid_cols, 0, 0),
            (1, bands, 1, band_rows, width),
        ).reshape(block, width)
        pieces.append(jnp.where(my_filled[k] > 0, piece, jnp.zeros_like(piece)))
    col_piece = jnp.stack(pieces)
    gathered = lax.all_gather(col_piece, "dp", axis=2, tiled=True)
    row_piece = lax.dynamic_slice_in_dim(gathered, column_group * width, width, 1)

    turned_right = jnp.einsum(
        "skj,sjc->skc", gathered, right, preferred_element_type=f32
    ).astype(bf16)
    turned = jnp.einsum("ski,skc->sic", left_full, turned_right, preferred_element_type=f32)
    new_first = 0.9 * first_adam_moment + 0.1 * turned
    new_second = 0.999 * second_adam_moment + 0.001 * turned * turned
    direction = (new_first / (jnp.sqrt(new_second) + 1e-08)).astype(bf16)
    mixed = jnp.einsum("sik,skc->sic", left_full, direction, preferred_element_type=f32).astype(bf16)
    partial = jnp.einsum(
        "sic,sdjc->dsij",
        mixed,
        right.reshape(per_owner, replicas, width, width),
        preferred_element_type=f32,
    ).astype(bf16)
    new_left = 0.95 * left_statistic_matrix + 0.05 * jnp.einsum(
        "sik,sjk->sij", gathered, row_piece, preferred_element_type=f32
    )
    new_right = 0.95 * right_statistic_matrix + 0.05 * jnp.einsum(
        "ski,skj->sij", gathered, col_piece, preferred_element_type=f32
    )

    back = lax.psum_scatter(
        partial.reshape(replicas * per_owner * block, width), "dp", scatter_dimension=0, tiled=True
    ).reshape(per_owner, bands, band_rows, width)

    placed = []
    for cell in range(cells):
        here = jnp.zeros((bands, band_rows, width), bf16)
        for k in range(per_owner):
            here = jnp.where((my_filled[k] > 0) & (my_cell[k] == cell), back[k], here)
        placed.append(here)
    placed = jnp.stack(placed).reshape(grid_rows, grid_cols, bands, band_rows, width)
    placed = jnp.transpose(placed, (0, 2, 1, 3, 4)).reshape(members * grid_cols * band_rows, width)
    mine = lax.psum_scatter(placed, "fsdp", scatter_dimension=0, tiled=True)
    update = jnp.transpose(mine.reshape(grid_cols, band_rows, width), (1, 0, 2))
    return (new_left, new_right, new_first, new_second, update)


def solution(mesh):
    slots = P("fsdp", None, "dp")
    in_specs = (P("dp", "fsdp", None, None), P(), P()) + (slots,) * 6
    return jax.shard_map(
        local, mesh=mesh, in_specs=in_specs, out_specs=(slots,) * 5, check_vma=False
    )
```

```python
import functools

import jax
import jax.numpy as jnp
from jax import lax
from jax.experimental import pallas as pl
from jax.experimental.pallas import tpu as pltpu
from jax.sharding import PartitionSpec as P

MESH = pl.DeviceIdType.MESH


def meet(replicas, members, d, m):
    barrier = pltpu.get_barrier_semaphore()
    for o in range(1, replicas):
        pl.semaphore_signal(
            barrier, inc=1, device_id={"dp": lax.rem(d + o, replicas)}, device_id_type=MESH
        )
    for o in range(1, members):
        pl.semaphore_signal(
            barrier, inc=1, device_id={"fsdp": lax.rem(m + o, members)}, device_id_type=MESH
        )
    pl.semaphore_wait(barrier, replicas + members - 2)


def push(src, dst, send, recv, axis, to):
    copy = pltpu.make_async_remote_copy(
        src_ref=src,
        dst_ref=dst,
        send_sem=send,
        recv_sem=recv,
        device_id={axis: to},
        device_id_type=MESH,
    )
    copy.start()
    return copy


def spread_first(full, mine, d, sems):
    width = mine.shape[1]
    here = full.at[:, pl.ds(pl.multiple_of(d * width, width), width)]
    own = pltpu.make_async_copy(mine, here, sems.at[2, 0])
    own.start()
    one = push(mine, here, sems.at[0, 0], sems.at[1, 0], "dp", d + 1 - 2 * lax.rem(d, 2))
    two = push(mine, here, sems.at[0, 1], sems.at[1, 1], "dp", lax.rem(d + 2, 4))
    return own, one, two


def spread_relay(full, width, d, sems, first):
    half = full.shape[0] // 2
    d1 = d + 1 - 2 * lax.rem(d, 2)
    d2 = lax.rem(d + 2, 4)
    first[1].wait_recv()
    top = full.at[pl.ds(0, half), pl.ds(pl.multiple_of(d1 * width, width), width)]
    a = push(top, top, sems.at[0, 2], sems.at[1, 2], "dp", d2)
    first[2].wait_recv()
    low = full.at[pl.ds(half, half), pl.ds(pl.multiple_of(d2 * width, width), width)]
    b = push(low, low, sems.at[0, 3], sems.at[1, 3], "dp", d1)
    return a, b


def step_kernel(
    replicas, members, pick_ref, fill_ref, at_ref, terms, left, right, lstat, rstat, first, second,
    new_left, new_right, new_first, new_second, upd,
    gath, leftf, col, xs, red, p1, p0, rs0, s0, g2, gs, ls, rf, rb, tr, dr, partial, ina, inb, rel, ina2, inb2, bk, h1, p2, ld, rs, s1, s2,
):
    d, m = lax.axis_index("dp"), lax.axis_index("fsdp")
    per_owner, block, width = right.shape
    grid_cols, piece = upd.shape[1:3]
    bands = block // (members * piece)
    hb, half = bands // 2, block // 2
    f32, bf16 = jnp.float32, jnp.bfloat16
    d1 = d + 1 - 2 * lax.rem(d, 2)
    d2 = lax.rem(d + 2, 4)
    d3 = 3 - d
    loads = [
        pltpu.make_async_copy(s, t, ld.at[i])
        for i, (s, t) in enumerate(
            (
                (right, rf), (first, new_first), (second, new_second),
                (lstat, new_left), (rstat, new_right),
            )
        )
    ]
    for c in loads:
        c.start()
    meet(replicas, members, d, m)
    tiles = block // width
    mine = pl.ds(pl.multiple_of(d * width, width), width)

    def mul(x, y, dims):
        return lax.dot_general(x, y, (dims, ((), ())), preferred_element_type=f32)

    def tile(i):
        return pl.ds(pl.multiple_of(i * width, width), width)

    def turn(k):
        @pl.loop(0, tiles)
        def _(i):
            tr[tile(i)] = mul(gath[k, tile(i)], rb[k], ((1,), (0,))).astype(bf16)

        @pl.loop(0, tiles)
        def _(i):
            t = mul(leftf[k, :, tile(i)], tr[...], ((0,), (0,)))
            nf = 0.9 * new_first[k, tile(i)] + 0.1 * t
            ns = 0.999 * new_second[k, tile(i)] + 0.001 * t * t
            new_first[k, tile(i)] = nf
            new_second[k, tile(i)] = ns
            dr[tile(i)] = (nf / (jnp.sqrt(ns) + 1e-08)).astype(bf16)

        @pl.loop(0, tiles)
        def _(i):
            x = mul(leftf[k, tile(i)], dr[...], ((1,), (0,))).astype(bf16)
            for t in range(replicas):
                partial[t, k, tile(i)] = mul(
                    x, rb[k, t * width : (t + 1) * width], ((1,), (1,))
                ).astype(bf16)

    def stats(k):
        @pl.loop(0, tiles)
        def _(i):
            a = mul(gath[k, tile(i)], gath[k, mine], ((1,), (1,)))
            new_left[k, tile(i)] = 0.95 * new_left[k, tile(i)] + 0.05 * a
            c = mul(gath[k, :, tile(i)], gath[k, :, mine], ((0,), (0,)))
            new_right[k, tile(i)] = 0.95 * new_right[k, tile(i)] + 0.05 * c

    top, low = pl.ds(0, half), pl.ds(half, half)

    def launch(k):
        return [
            push(partial.at[d3, k, top], ina.at[k, 1], rs.at[0, k, 0], rs.at[1, k, 0], "dp", d1),
            push(partial.at[d3, k, low], inb.at[k, 1], rs.at[0, k, 1], rs.at[1, k, 1], "dp", d2),
            push(partial.at[d1, k, top], ina.at[k, 0], rs.at[0, k, 2], rs.at[1, k, 2], "dp", d1),
            push(partial.at[d2, k, low], inb.at[k, 0], rs.at[0, k, 3], rs.at[1, k, 3], "dp", d2),
        ]

    def relay(k, c):
        c[0].wait_recv()
        rel[k, 0] = (partial[d2, k, top].astype(f32) + ina[k, 1].astype(f32)).astype(bf16)
        a = push(rel.at[k, 0], ina2.at[k], rs.at[0, k, 4], rs.at[1, k, 4], "dp", d2)
        c[1].wait_recv()
        rel[k, 1] = (partial[d1, k, low].astype(f32) + inb[k, 1].astype(f32)).astype(bf16)
        b = push(rel.at[k, 1], inb2.at[k], rs.at[0, k, 5], rs.at[1, k, 5], "dp", d1)
        return [a, b]

    out, out2 = [], []

    def finish(k, c, r):
        for h in range(2):
            c[2 + h].wait_recv()
            r[h].wait_recv()
            near, far = ((ina, ina2), (inb, inb2))[h]
            for p in range(members):
                to = lax.rem(m + p, members)
                at = (m * per_owner + k) * bands + h * hb
                for q in range(hb):
                    row = pl.ds(pl.multiple_of((q * members + to) * piece, piece), piece)
                    own = pl.ds(pl.multiple_of(h * half + (q * members + to) * piece, piece), piece)
                    acc = (
                        partial[d, k, own].astype(f32)
                        + near[k, 0, row].astype(f32)
                        + far[k, row].astype(f32)
                    ).astype(bf16)
                    if p:
                        bk[k, h, to, q] = acc
                    else:
                        h1[at + q] = acc
                if p:
                    out.append(
                        push(
                            bk.at[k, h, to], h1.at[pl.ds(at, hb)],
                            s1.at[0, k, h, p], s1.at[1, k, h, p], "fsdp", to,
                        )
                    )

    hm = members // 2
    upper, lower = pl.ds(0, hm), pl.ds(hm, hm)
    g = [
        push(terms.at[d3, upper], xs.at[1, upper], rs0.at[0, 0], rs0.at[1, 0], "dp", d1),
        push(terms.at[d3, lower], xs.at[1, lower], rs0.at[0, 1], rs0.at[1, 1], "dp", d2),
        push(terms.at[d1, upper], xs.at[0, upper], rs0.at[0, 2], rs0.at[1, 2], "dp", d1),
        push(terms.at[d2, lower], xs.at[0, lower], rs0.at[0, 3], rs0.at[1, 3], "dp", d2),
    ]
    g[0].wait_recv()
    xs[2, upper] = (terms[d2, upper].astype(f32) + xs[1, upper].astype(f32)).astype(bf16)
    g.append(push(xs.at[2, upper], xs.at[3, upper], rs0.at[0, 4], rs0.at[1, 4], "dp", d2))
    g[1].wait_recv()
    xs[2, lower] = (terms[d1, lower].astype(f32) + xs[1, lower].astype(f32)).astype(bf16)
    g.append(push(xs.at[2, lower], xs.at[3, lower], rs0.at[0, 5], rs0.at[1, 5], "dp", d1))
    for c in g[2:]:
        c.wait_recv()
    spread = []
    for p in range(members):
        to = lax.rem(m + p, members)
        acc = terms[d, to].astype(f32) + xs[0, to].astype(f32) + xs[3, to].astype(f32)
        here = pl.ds(m * grid_cols, grid_cols)
        if p:
            red[to] = acc.astype(bf16)
            spread.append(push(red.at[to], p1.at[here], s0.at[0, p], s0.at[1, p], "fsdp", to))
        else:
            p1[here] = acc.astype(bf16)
    lfirst = [spread_first(leftf.at[k], left.at[k], d, ls.at[k]) for k in range(per_owner)]
    loads[0].wait()
    rb[...] = rf[...].astype(bf16)
    for c in spread:
        c.wait_recv()
    dealt = []
    for k in range(per_owner):
        dealt.append([])
        for p in range(members):
            to = lax.rem(m + p, members)
            keep = fill_ref[to * per_owner + k]
            for b in range(bands):
                got = p1[pick_ref[(to * per_owner + k) * bands + b]]
                got = (got.astype(f32) * keep).astype(bf16)
                if p:
                    p0[to, k, b] = got
                else:
                    col[k, b, m] = got
            if p:
                dealt[k].append(
                    push(
                        p0.at[to, k], col.at[k, :, m],
                        g2.at[0, k, p], g2.at[1, k, p], "fsdp", to,
                    )
                )
    lrelay = [
        spread_relay(leftf.at[k], width, d, ls.at[k], lfirst[k]) for k in range(per_owner)
    ]
    gfirst = []
    for k in range(per_owner):
        for c in dealt[k]:
            c.wait_recv()
        gfirst.append(
            spread_first(gath.at[k], col.at[k].reshape(block, width), d, gs.at[k])
        )
    grelay = [
        spread_relay(gath.at[k], width, d, gs.at[k], gfirst[k]) for k in range(per_owner)
    ]
    loads[1].wait()
    loads[2].wait()
    sent, passed = [], []
    for k in range(per_owner):
        lfirst[k][0].wait()
        gfirst[k][0].wait()
        for c in lrelay[k] + grelay[k]:
            c.wait_recv()
        turn(k)
        sent.append(launch(k))
    loads[3].wait()
    loads[4].wait()
    for k in range(per_owner):
        stats(k)
        passed.append(relay(k, sent[k]))
    for k in range(per_owner):
        finish(k, sent[k], passed[k])
    for c in out:
        c.wait_recv()
    for p in range(members):
        to = lax.rem(m + p, members)
        for c in range(grid_cols):
            got = h1[at_ref[to * grid_cols + c]]
            if p:
                p2[to, c] = got
            else:
                upd[m, c] = got
        if p:
            out2.append(push(p2.at[to], upd.at[m], s2.at[0, p], s2.at[1, p], "fsdp", to))
    for c in out2:
        c.wait_recv()
    for c in g + spread + sum(dealt + sent + passed, []) + out + out2:
        c.wait_send()
    for k in range(per_owner):
        for c in lfirst[k][1:] + lrelay[k] + gfirst[k][1:] + grelay[k]:
            c.wait_send()


def step(pick, fill, at, terms, left, right, lstat, rstat, first, second):
    per_owner, block, width = right.shape
    replicas, members, grid_cols, piece, _ = terms.shape
    bands = block // (members * piece)
    bf16, f32, dma = jnp.bfloat16, jnp.float32, pltpu.SemaphoreType.DMA
    vmem = pl.BlockSpec(memory_space=pltpu.VMEM)
    whole = pl.BlockSpec(memory_space=pl.ANY)
    state = jax.ShapeDtypeStruct(right.shape, f32)
    half = (per_owner, 2, block // 2, width)
    return pl.pallas_call(
        functools.partial(step_kernel, replicas, members),
        out_shape=(state,) * 4
        + (jax.ShapeDtypeStruct((members, grid_cols, piece, width), bf16),),
        in_specs=[pl.BlockSpec(memory_space=pltpu.SMEM)] * 3 + [vmem] * 2 + [whole] * 5,
        out_specs=(vmem,) * 5,
        scratch_shapes=[
            pltpu.VMEM((per_owner, block, replicas * width), bf16),
            pltpu.VMEM((per_owner, block, replicas * width), bf16),
            pltpu.VMEM((per_owner, bands, members, piece, width), bf16),
            pltpu.VMEM((4,) + terms.shape[1:], bf16),
            pltpu.VMEM(terms.shape[1:], bf16),
            pltpu.VMEM((members * grid_cols, piece, width), bf16),
            pltpu.VMEM((members, per_owner, bands, piece, width), bf16),
            dma((2, 6)), dma((2, members)), dma((2, per_owner, members)),
            dma((per_owner, 3, 4)), dma((per_owner, 3, 4)),
            pltpu.VMEM(right.shape, f32),
            pltpu.VMEM(right.shape, bf16),
            pltpu.VMEM((block, width), bf16),
            pltpu.VMEM((block, width), bf16),
            pltpu.VMEM((replicas, per_owner, block, width), bf16),
            pltpu.VMEM(half, bf16),
            pltpu.VMEM(half, bf16),
            pltpu.VMEM(half, bf16),
            pltpu.VMEM((per_owner, block // 2, width), bf16),
            pltpu.VMEM((per_owner, block // 2, width), bf16),
            pltpu.VMEM((per_owner, 2, members, bands // 2, piece, width), bf16),
            pltpu.VMEM((members * per_owner * bands, piece, width), bf16),
            pltpu.VMEM((members, grid_cols, piece, width), bf16),
            dma((5,)), dma((2, per_owner, 6)), dma((2, per_owner, 2, members)), dma((2, members)),
        ],
        compiler_params=pltpu.CompilerParams(
            collective_id=0, has_side_effects=True, vmem_limit_bytes=52 * 2**20
        ),
    )(pick, fill, at, terms, left, right, lstat, rstat, first, second)


def slot_lookup_table(block_owner_index, block_grid_cell, slot_count, per_owner):
    block_ids = jnp.arange(block_owner_index.shape[0], dtype=jnp.int32)
    shared = (block_owner_index[:, None] == block_owner_index[None, :]) & (
        block_ids[None, :] < block_ids[:, None]
    )
    rank_in = jnp.sum(shared.astype(jnp.int32), axis=1)
    block_slot_index = block_owner_index * per_owner + rank_in
    slot_ids = jnp.arange(slot_count, dtype=jnp.int32)
    matches = (block_slot_index[None, :] == slot_ids[:, None]).astype(jnp.int32)
    filled_marker = jnp.sum(matches, axis=1)
    slot_grid_cell = jnp.sum(matches * block_grid_cell[None, :], axis=1)
    return (block_slot_index, filled_marker, slot_grid_cell)


def local(
    gradient,
    block_owner_index,
    block_grid_cell,
    left_eigen_basis,
    right_eigen_basis,
    left_statistic_matrix,
    right_statistic_matrix,
    first_adam_moment,
    second_adam_moment,
):
    bf16, f32 = jnp.bfloat16, jnp.float32
    replicas = lax.axis_size("dp")
    members = lax.axis_size("fsdp")
    member = lax.axis_index("fsdp")
    column_group = lax.axis_index("dp")
    per_owner, block, width = left_eigen_basis.shape
    band_rows, grid_cols = gradient.shape[1:3]
    bands = block // band_rows
    grid_rows = members // bands
    cells = grid_rows * grid_cols

    block_slot_index, filled_marker, slot_grid_cell = slot_lookup_table(
        block_owner_index, block_grid_cell, per_owner * members, per_owner
    )
    my_filled = lax.dynamic_slice_in_dim(filled_marker, member * per_owner, per_owner, 0)
    my_cell = lax.dynamic_slice_in_dim(slot_grid_cell, member * per_owner, per_owner, 0)

    left = left_eigen_basis.astype(bf16)
    right = right_eigen_basis.astype(bf16)
    piece_rows = band_rows // members
    direct = (
        replicas == 4 and bands % 2 == members % 2 == 0 and band_rows % members == 0 and piece_rows % 16 == 0
    )
    if direct:
        terms = jnp.transpose(
            gradient.reshape(members, piece_rows, grid_cols, replicas, width), (3, 0, 2, 1, 4)
        )
        part = jnp.arange(bands, dtype=jnp.int32)[None, :]
        pick = (
            (slot_grid_cell // grid_cols * bands)[:, None] + part
        ) * grid_cols + (slot_grid_cell % grid_cols)[:, None]
        all_cells = jnp.arange(cells, dtype=jnp.int32)
        hits = (block_grid_cell[None, :] == all_cells[:, None]).astype(jnp.int32)
        cell_slot = jnp.sum(hits * block_slot_index[None, :], axis=1)
        at = cell_slot.reshape(grid_rows, 1, grid_cols) * bands + jnp.arange(
            bands, dtype=jnp.int32
        ).reshape(1, bands, 1)
        *states, mine = step(
            pick.reshape(-1),
            (filled_marker > 0).astype(f32),
            at.reshape(-1),
            terms,
            left,
            right_eigen_basis,
            left_statistic_matrix,
            right_statistic_matrix,
            first_adam_moment,
            second_adam_moment,
        )
        update = jnp.transpose(mine, (0, 2, 1, 3)).reshape(band_rows, grid_cols, width)
        return (*states, update)
    left_full = lax.all_gather(left, "dp", axis=2, tiled=True)

    terms = jnp.transpose(
        gradient.reshape(band_rows, grid_cols, replicas, width), (2, 1, 0, 3)
    ).reshape(replicas * grid_cols * band_rows, width)
    reduced = lax.psum_scatter(terms, "dp", scatter_dimension=0, tiled=True)
    everyone = lax.all_gather(reduced, "fsdp", axis=0, tiled=True)
    everyone = everyone.reshape(grid_rows, bands, grid_cols, band_rows, width)
    pieces = []
    for k in range(per_owner):
        cell = my_cell[k]
        piece = lax.dynamic_slice(
            everyone,
            (cell // grid_cols, 0, cell % grid_cols, 0, 0),
            (1, bands, 1, band_rows, width),
        ).reshape(block, width)
        pieces.append(jnp.where(my_filled[k] > 0, piece, jnp.zeros_like(piece)))
    col_piece = jnp.stack(pieces)
    gathered = lax.all_gather(col_piece, "dp", axis=2, tiled=True)
    row_piece = lax.dynamic_slice_in_dim(gathered, column_group * width, width, 1)

    turned_right = jnp.einsum(
        "skj,sjc->skc", gathered, right, preferred_element_type=f32
    ).astype(bf16)
    turned = jnp.einsum("ski,skc->sic", left_full, turned_right, preferred_element_type=f32)
    new_first = 0.9 * first_adam_moment + 0.1 * turned
    new_second = 0.999 * second_adam_moment + 0.001 * turned * turned
    direction = (new_first / (jnp.sqrt(new_second) + 1e-08)).astype(bf16)
    mixed = jnp.einsum("sik,skc->sic", left_full, direction, preferred_element_type=f32).astype(bf16)
    partial = jnp.einsum(
        "sic,sdjc->dsij",
        mixed,
        right.reshape(per_owner, replicas, width, width),
        preferred_element_type=f32,
    ).astype(bf16)
    new_left = 0.95 * left_statistic_matrix + 0.05 * jnp.einsum(
        "sik,sjk->sij", gathered, row_piece, preferred_element_type=f32
    )
    new_right = 0.95 * right_statistic_matrix + 0.05 * jnp.einsum(
        "ski,skj->sij", gathered, col_piece, preferred_element_type=f32
    )

    back = lax.psum_scatter(
        partial.reshape(replicas * per_owner * block, width), "dp", scatter_dimension=0, tiled=True
    ).reshape(per_owner, bands, band_rows, width)

    placed = []
    for cell in range(cells):
        here = jnp.zeros((bands, band_rows, width), bf16)
        for k in range(per_owner):
            here = jnp.where((my_filled[k] > 0) & (my_cell[k] == cell), back[k], here)
        placed.append(here)
    placed = jnp.stack(placed).reshape(grid_rows, grid_cols, bands, band_rows, width)
    placed = jnp.transpose(placed, (0, 2, 1, 3, 4)).reshape(members * grid_cols * band_rows, width)
    mine = lax.psum_scatter(placed, "fsdp", scatter_dimension=0, tiled=True)
    update = jnp.transpose(mine.reshape(grid_cols, band_rows, width), (1, 0, 2))
    return (new_left, new_right, new_first, new_second, update)


def solution(mesh):
    slots = P("fsdp", None, "dp")
    in_specs = (P("dp", "fsdp", None, None), P(), P()) + (slots,) * 6
    return jax.shard_map(
        local, mesh=mesh, in_specs=in_specs, out_specs=(slots,) * 5, check_vma=False
    )
```
